32 devices in a mesh: blocks: 2 (over y), rows: 4 (over z), cols: 4 (over x, core).
Axes of the slice: x: 2, y: 2, z: 4, core: 2. Of those that a mesh axis runs over, the one named last changes fastest.
Arguments:
- sens_tiles: bfloat16 [128, 1024, 256], P(('blocks', 'rows'), 'cols'), parts along dimension 0, may hold values from -10.606602 to 10.606602, as said below
- tile_coords: int32 [128, 8], P(('blocks', 'rows'), 'cols'), parts along dimension 0, may hold values from 0 to 7, as said below
- tile_counts: int32 [8, 4], P(('blocks', 'rows'), 'cols'), parts along dimension 0, may hold values from 3 to 16, as said below
- data_vec: float32 [192, 4096], P('blocks', 'rows'), parts along dimension 0, may hold values from -6 to 6
- cell_vec: float32 [192, 8192], P('blocks', 'cols'), parts along dimension 0, may hold values from -6 to 6
- alpha_now: float32 [192], P('blocks'), parts along dimension 0, may hold values from 0.5 to 2
Outputs:
- data_next: float32 [192, 4096], P('blocks', 'rows'), parts along dimension 0
- cell_next: float32 [192, 8192], P('blocks', 'cols'), parts along dimension 0
- beta_next: float32 [192], P('blocks'), parts along dimension 0
- alpha_next: float32 [192], P('blocks'), parts along dimension 0
The draws below stay inside these ranges and needn't reach their ends.
There are 2 independent parts, one for each index of `blocks`. The reference program is written for one: setup_inputs(seed, part) draws one part's arguments, and reference() takes and returns one part's arrays. A program takes and returns all parts, laid end to end along the dimension named above; each array names one. Nothing has to cross between parts.
Inputs may be any that keep to these rules, and one draw needn't show every extreme that they name: `sens_tiles`: entries of the tiles; slots at or beyond a device's count hold values that belong to no tile. `tile_coords`: within one device all 16 slots name distinct (row tile, column tile) pairs; the first entry of a pair is below 4, the second below 8. `tile_counts`: every data-row band has one device whose count is 16.
All inputs are finite; a program needn't handle non-finite values.
Results may differ from the reference program's by a relative error of at most 0.0043.
Values sent between devices are 32-bit elements; how exact they have to be, the bound alone decides.
A program may use at most 64 MiB of HBM per device.

```python
import math
import jax
import jax.numpy as jnp
from jax import lax

TILE = 256
RT = 4
CT = 8
TMAX = 16
SAMPLES = 96
ROW_BANDS = 4
COL_BANDS = 4
DATA = 4096
CELLS = 8192


def draw_sens_tiles(key, part):
    rows_total = ROW_BANDS * TMAX
    key_noise, key_rows, key_cols = jax.random.split(key, 3)
    shape_four = (rows_total, COL_BANDS, TILE, TILE)
    noise = jnp.clip(jax.random.normal(key_noise, shape_four, jnp.float32), -6.0, 6.0)
    lowest, highest = (0.3, 3.0)
    row_scale = jnp.exp(jax.random.uniform(key_rows, (rows_total, COL_BANDS, TILE, 1), jnp.float32, math.log(lowest), math.log(highest)))
    col_scale = jnp.exp(jax.random.uniform(key_cols, (rows_total, COL_BANDS, 1, TILE), jnp.float32, math.log(lowest), math.log(highest)))
    row_band = (jnp.arange(rows_total) // TMAX).astype(jnp.float32) / max(ROW_BANDS - 1, 1)
    col_band = jnp.arange(COL_BANDS).astype(jnp.float32) / max(COL_BANDS - 1, 1)
    band_factor = 3.0 ** (0.5 * (row_band[:, None] + col_band[None, :]))
    values = noise * row_scale * col_scale * band_factor[:, :, None, None] / math.sqrt(TILE * CT)
    return values.reshape(rows_total, COL_BANDS * TILE, TILE).astype(jnp.bfloat16)


def draw_tile_coords(key, part):
    device_keys = jax.random.split(key, ROW_BANDS * COL_BANDS)
    orders = jax.vmap(lambda one_key: jax.random.permutation(one_key, RT * CT))(device_keys)[:, :TMAX]
    stacked = jnp.stack([orders // CT, orders % CT], axis=-1)
    stacked = stacked.reshape(ROW_BANDS, COL_BANDS, TMAX, 2).transpose(0, 2, 1, 3)
    return stacked.reshape(ROW_BANDS * TMAX, COL_BANDS * 2).astype(jnp.int32)


def draw_tile_counts(key, part):
    key_base, key_full = jax.random.split(key, 2)
    base = jax.random.randint(key_base, (ROW_BANDS, COL_BANDS), TMAX // 8 + 1, TMAX * 5 // 8 + 1, jnp.int32)
    chosen = jax.random.randint(key_full, (ROW_BANDS, 1), 0, COL_BANDS, jnp.int32)
    columns = jnp.arange(COL_BANDS, dtype=jnp.int32)[None, :]
    return jnp.where(columns == chosen, TMAX, base).astype(jnp.int32)


def block_levels(key, shape, cuts, smallest, top_value):
    def one(position, parts):
        steps = jax.random.uniform(jax.random.fold_in(jax.random.fold_in(key, 6), position), (parts,), jnp.float32, smallest / len(cuts), top_value / len(cuts))
        return jnp.repeat(jnp.exp(steps), shape[position] // parts).reshape((-1,) + (1,) * (len(shape) - position - 1))

    factor_of = one(*cuts[0])
    for cut in cuts[1:]:
        factor_of = factor_of * one(*cut)
    return factor_of


def bell_draw(stream_key, extent, scale, bound, cuts=(), held_as=jnp.bfloat16):
    level = block_levels(stream_key, extent, cuts, -0.22, 0.18) if cuts else 1.0
    entries = jax.random.normal(stream_key, extent, jnp.float32) * scale * level
    return jnp.minimum(jnp.maximum(entries, -bound), bound).astype(held_as)


def setup_inputs(seed: int = 0, part: int = 0) -> dict:
    arg_keys = jax.random.split(jax.random.key(seed), 7)
    part_splits = jax.random.split(jax.random.fold_in(arg_keys[6], part), 7)
    sens_tiles = draw_sens_tiles(jax.random.fold_in(jax.random.fold_in(arg_keys[6], part), 71), part)
    tile_coords = draw_tile_coords(jax.random.fold_in(jax.random.fold_in(arg_keys[6], part), 71), part)
    tile_counts = draw_tile_counts(jax.random.fold_in(jax.random.fold_in(arg_keys[6], part), 71), part)
    data_vec = bell_draw(part_splits[3], (SAMPLES, DATA), 1.0, 6.0, ((1, 4),), jnp.float32)
    cell_vec = bell_draw(part_splits[4], (SAMPLES, CELLS), 1.0, 6.0, ((1, 4),), jnp.float32)
    alpha_now = jnp.clip(jnp.exp(jax.random.uniform(part_splits[5], (SAMPLES,), jnp.float32, math.log(0.5), math.log(2.0))), 0.5, 2.0)
    return {"sens_tiles": sens_tiles, "tile_coords": tile_coords, "tile_counts": tile_counts, "data_vec": data_vec, "cell_vec": cell_vec, "alpha_now": alpha_now}


EPSILON = 1e-06

def arrange(sens_tiles, tile_coords, tile_counts):
    layered = sens_tiles.reshape(ROW_BANDS, TMAX, COL_BANDS, TILE, TILE).transpose(0, 2, 1, 3, 4)
    places = tile_coords.reshape(ROW_BANDS, TMAX, COL_BANDS, 2).transpose(0, 2, 1, 3)
    listed = (jnp.arange(TMAX, dtype=jnp.int32)[None, None, :] < tile_counts[:, :, None]).astype(jnp.float32)
    return (layered, places, listed)

def forward_product(layered, places, listed, cell_low):
    cell_blocks = cell_low.astype(jnp.float32).reshape(SAMPLES, COL_BANDS, CT, TILE)

    def one_band(operands):
        band_tiles, band_places, band_listed = operands
        picked = jnp.take_along_axis(cell_blocks, band_places[None, :, :, 1, None].astype(jnp.int32), axis=2)
        contrib = jnp.einsum('kctj,ctij->kcti', picked, band_tiles.astype(jnp.float32), precision=lax.Precision.HIGHEST)
        spread = jax.nn.one_hot(band_places[:, :, 0], RT, dtype=jnp.float32) * band_listed[:, :, None]
        return jnp.einsum('kcti,ctr->kri', contrib, spread, precision=lax.Precision.HIGHEST)
    banded = lax.map(one_band, (layered, places, listed))
    return banded.transpose(1, 0, 2, 3).reshape(SAMPLES, ROW_BANDS * RT * TILE)

def adjoint_product(layered, places, listed, data_low):
    row_blocks = data_low.astype(jnp.float32).reshape(SAMPLES, ROW_BANDS, RT, TILE).transpose(1, 0, 2, 3)

    def one_band(running, operands):
        band_rows, band_tiles, band_places, band_listed = operands
        picked = jnp.take(band_rows, band_places[:, :, 0].astype(jnp.int32), axis=1)
        contrib = jnp.einsum('kcti,ctij->kctj', picked, band_tiles.astype(jnp.float32), precision=lax.Precision.HIGHEST)
        spread = jax.nn.one_hot(band_places[:, :, 1], CT, dtype=jnp.float32) * band_listed[:, :, None]
        return (running + jnp.einsum('kctj,cts->kcsj', contrib, spread, precision=lax.Precision.HIGHEST), None)
    empty_sum = jnp.zeros((SAMPLES, COL_BANDS, CT, TILE), jnp.float32)
    running, _ = lax.scan(one_band, empty_sum, (row_blocks, layered, places, listed))
    return running.reshape(SAMPLES, COL_BANDS * CT * TILE)

def reference(sens_tiles, tile_coords, tile_counts, data_vec, cell_vec, alpha_now):
    layered, places, listed = arrange(sens_tiles, tile_coords, tile_counts)
    forward = forward_product(layered, places, listed, cell_vec.astype(jnp.bfloat16))
    residual = forward - alpha_now[:, None] * data_vec
    beta_next = jnp.sqrt(lax.optimization_barrier(jnp.sum(residual * residual, axis=1)) / DATA + EPSILON)
    data_next = residual / beta_next[:, None]
    backward = adjoint_product(layered, places, listed, data_next.astype(jnp.bfloat16))
    fresh = backward - beta_next[:, None] * cell_vec
    alpha_next = jnp.sqrt(lax.optimization_barrier(jnp.sum(fresh * fresh, axis=1)) / CELLS + EPSILON)
    cell_next = fresh / alpha_next[:, None]
    return (data_next, cell_next, beta_next, alpha_next)
```

```python
import functools

import jax
import jax.numpy as jnp
from jax import lax
from jax.experimental import pallas as pl
from jax.experimental.pallas import tpu as pltpu
from jax.sharding import PartitionSpec as P

EPSILON = 1e-06
MESH = pl.DeviceIdType.MESH
CHUNK = 256


def remote(src, dst, send_sem, recv_sem, axis, peer):
    return pltpu.make_async_remote_copy(
        src_ref=src, dst_ref=dst, send_sem=send_sem, recv_sem=recv_sem, device_id={axis: peer}, device_id_type=MESH
    )


class Line:
    def __init__(self, count, place, axis, device_of, own, up, down, up_out, down_out, sems):
        self.count, self.place, self.axis, self.device_of = count, place, axis, device_of
        self.own, self.up, self.down, self.up_out, self.down_out = own, up, down, up_out, down_out
        self.up_send, self.up_recv, self.down_send, self.down_recv = sems
        self.chunks = own.shape[0]

    def up_copy(self, src, i):
        peer = self.device_of(lax.rem(self.place + 1, self.count))
        return remote(src.at[i], self.up.at[i], self.up_send.at[i], self.up_recv.at[i], self.axis, peer)

    def down_copy(self, src, i):
        peer = self.device_of(lax.rem(self.place + self.count - 1, self.count))
        return remote(src.at[i], self.down.at[i], self.down_send.at[i], self.down_recv.at[i], self.axis, peer)

    def begin(self, i):
        @pl.when(self.place == 0)
        def _():
            self.up_copy(self.own, i).start()

        @pl.when(self.place == self.count - 1)
        def _():
            self.down_copy(self.own, i).start()

    def run(self, finish):
        first, last = self.place == 0, self.place == self.count - 1
        from_below = self.place
        from_above = self.count - 1 - self.place

        def slot(s, carry):
            i = s - from_below

            @pl.when(jnp.logical_not(first) & (i >= 0) & (i < self.chunks))
            def _():
                self.up_copy(self.up_out, i).wait_recv()

                @pl.when(jnp.logical_not(last))
                def _():
                    self.up_out[i] = self.own[i] + self.up[i]
                    self.up_copy(self.up_out, i).start()

            k = s - from_above

            @pl.when(jnp.logical_not(last) & (k >= 0) & (k < self.chunks))
            def _():
                self.down_copy(self.down_out, k).wait_recv()

                @pl.when(jnp.logical_not(first))
                def _():
                    self.down_out[k] = self.own[k] + self.down[k]
                    self.down_copy(self.down_out, k).start()

            m = s - jnp.maximum(from_below, from_above)

            @pl.when((m >= 0) & (m < self.chunks))
            def _():
                @pl.when(first)
                def _():
                    finish(m, self.own[m] + self.down[m])

                @pl.when(last)
                def _():
                    finish(m, self.up[m] + self.own[m])

                if self.count > 2:

                    @pl.when(jnp.logical_not(first | last))
                    def _():
                        finish(m, self.up_out[m] + self.down[m])

            return carry

        lax.fori_loop(0, self.chunks + self.count - 1, slot, 0)

    def end(self):
        def one(i, carry):
            @pl.when(self.place < self.count - 1)
            def _():
                self.up_copy(self.own, i).wait_send()

            @pl.when(self.place > 0)
            def _():
                self.down_copy(self.own, i).wait_send()

            return carry

        lax.fori_loop(0, self.chunks, one, 0)


def share_start(axis, count, me, row, out, got, send, recv):
    wide = jnp.broadcast_to(row, out.shape)
    out[...] = wide
    got[me] = wide

    def one(d, carry):
        peer = lax.rem(me + d, count)
        remote(out, got.at[me], send.at[d], recv.at[me], axis, peer).start()
        return carry

    lax.fori_loop(1, count, one, 0)


def share_end(axis, count, me, out, got, send, recv):
    def one(d, carry):
        peer = lax.rem(me + d, count)
        remote(out, got.at[peer], send.at[d], recv.at[peer], axis, peer).wait_recv()
        return carry

    lax.fori_loop(1, count, one, 0)

    def sent(d, carry):
        peer = lax.rem(me + d, count)
        remote(out, got.at[me], send.at[d], recv.at[me], axis, peer).wait_send()
        return carry

    lax.fori_loop(1, count, sent, 0)
    total = got[0]
    for j in range(1, count):
        total = total + got[j]
    return total[0:1]


def kernel(
    rows, cols,
    coords, counts, alpha_in, tiles_in, data_in, cell_in,
    data_out, cell_out, beta_out, alpha_out,
    table, keys, tiles, data, cell, cell_low, other, other_got, half, half_up, half_down, half_up_out, half_down_out,
    resid, resid_low, part, part_up, part_down, part_up_out, part_down_out, squares,
    beta_row, beta_got, alpha_row, alpha_got,
    load_sems, pair_send, pair_recv, back_send, back_recv, half_sems, part_sems, beta_sems, alpha_sems,
):
    slots, tile = tiles_in.shape[0], tiles_in.shape[1]
    samples = data_in.shape[0]
    row_tiles, col_tiles = data_in.shape[1] // tile, cell_in.shape[1] // tile
    halves = row_tiles // 2
    r, c = lax.axis_index("rows"), lax.axis_index("cols")
    side = lax.rem(c, 2)
    group = c // 2
    partner = c + 1 - 2 * side

    barrier = pltpu.get_barrier_semaphore()

    def greet(axis, count, me):
        def one(d, carry):
            pl.semaphore_signal(barrier, inc=1, device_id={axis: lax.rem(me + d, count)}, device_id_type=MESH)
            return carry

        lax.fori_loop(1, count, one, 0)

    greet("rows", rows, r)
    greet("cols", cols, c)

    loads = [
        pltpu.make_async_copy(cell_in, cell, load_sems.at[0]),
        pltpu.make_async_copy(tiles_in, tiles.at[pl.ds(0, slots)], load_sems.at[1]),
        pltpu.make_async_copy(data_in, data, load_sems.at[2]),
    ]
    for load in loads:
        load.start()
    tiles[slots] = jnp.zeros(tiles.shape[1:], tiles.dtype)

    listed = counts[0, 0]
    for t in range(slots):
        keys[t] = jnp.where(t < listed, coords[t, 0] * col_tiles + coords[t, 1], -1)

    def find(p, carry):
        found = jnp.int32(slots)
        for t in range(slots):
            found = jnp.where(keys[t] == p, t, found)
        table[p] = found
        return carry

    lax.fori_loop(0, row_tiles * col_tiles, find, 0)

    lanes = alpha_in.shape[1]
    eye = lax.broadcasted_iota(jnp.int32, (samples, lanes), 0) == lax.broadcasted_iota(jnp.int32, (samples, lanes), 1)

    def as_row(column):
        return jnp.sum(jnp.where(eye, column, 0.0), axis=0, keepdims=True)

    def as_column(row):
        return jnp.sum(jnp.where(eye, row, 0.0), axis=1, keepdims=True)

    alpha = as_column(alpha_in[...])

    loads[0].wait()
    for b in range(col_tiles):
        cell_low[b] = cell[:, b * tile:(b + 1) * tile].astype(jnp.bfloat16)
    loads[1].wait()

    def forward(a):
        total = None
        for b in range(col_tiles):
            term = lax.dot_general(
                cell_low[b], tiles[table[a * col_tiles + b]], (((1,), (1,)), ((), ())),
                preferred_element_type=jnp.float32,
            )
            total = term if total is None else total + term
        return total

    def pair_copy(j):
        return remote(other.at[j], other_got.at[j], pair_send.at[j], pair_recv.at[j], "cols", partner)

    other[0] = forward((1 - side) * halves)
    pl.semaphore_wait(barrier, rows + cols - 2)
    pair_copy(0).start()
    for j in range(1, halves):
        other[j] = forward((1 - side) * halves + j)
        pair_copy(j).start()

    across = Line(
        cols // 2, group, "cols", lambda q: q * 2 + side, half, half_up, half_down, half_up_out, half_down_out,
        [half_sems.at[i] for i in range(4)],
    )
    for j in range(halves):
        own = forward(side * halves + j)
        pair_copy(j).wait_recv()
        half[j] = own + other_got[j]
        across.begin(j)

    loads[2].wait()

    def back_copy(a, j):
        return remote(resid.at[a], resid.at[a], back_send.at[j], back_recv.at[j], "cols", partner)

    def finish_rows(j, total):
        a = side * halves + j
        here = pl.ds(pl.multiple_of(a * tile, tile), tile)
        resid[a] = total - alpha * data[:, here]
        back_copy(a, j).start()

    across.run(finish_rows)
    for j in range(halves):
        back_copy((1 - side) * halves + j, j).wait_recv()

    sums = jnp.zeros((samples, 1), jnp.float32)
    for a in range(row_tiles):
        block = resid[a]
        resid_low[a] = block.astype(jnp.bfloat16)
        sums = sums + jnp.sum(block * block, axis=1, keepdims=True)
    share_start("rows", rows, r, as_row(sums), beta_row, beta_got, beta_sems.at[0], beta_sems.at[1])

    along = Line(
        rows, r, "rows", lambda q: q, part, part_up, part_down, part_up_out, part_down_out,
        [part_sems.at[i] for i in range(4)],
    )
    width = part.shape[2]
    pieces = tile // width
    for b in range(col_tiles):
        total = None
        for a in range(row_tiles):
            term = jnp.dot(resid_low[a], tiles[table[a * col_tiles + b]], preferred_element_type=jnp.float32)
            total = term if total is None else total + term
        for e in range(pieces):
            part[b * pieces + e] = total[:, e * width:(e + 1) * width]
            along.begin(b * pieces + e)

    data_total = jnp.float32(data_in.shape[1] * rows)
    cell_total = jnp.float32(cell_in.shape[1] * cols)
    beta = jnp.sqrt(
        share_end("rows", rows, r, beta_row, beta_got, beta_sems.at[0], beta_sems.at[1]) / data_total + EPSILON
    )
    beta_out[...] = beta
    beta_column = as_column(beta)
    beta_inverse = 1.0 / beta_column
    for a in range(row_tiles):
        data_out[:, a * tile:(a + 1) * tile] = resid[a] * beta_inverse
    squares[...] = jnp.zeros_like(squares)

    def finish_cells(i, total):
        here = pl.ds(pl.multiple_of(i * width, width), width)
        fresh = total * beta_inverse - beta_column * cell[:, here]
        cell_out[:, here] = fresh
        square = fresh * fresh
        piece = square[:, :128]
        for e in range(1, width // 128):
            piece = piece + square[:, e * 128:(e + 1) * 128]
        squares[...] += piece

    along.run(finish_cells)
    sums = jnp.sum(squares[...], axis=1, keepdims=True)
    share_start("cols", cols, c, as_row(sums), alpha_row, alpha_got, alpha_sems.at[0], alpha_sems.at[1])
    for j in range(halves):
        pair_copy(j).wait_send()
        back_copy(side * halves + j, j).wait_send()
    across.end()
    along.end()
    alpha_next = jnp.sqrt(
        share_end("cols", cols, c, alpha_row, alpha_got, alpha_sems.at[0], alpha_sems.at[1]) / cell_total + EPSILON
    )
    alpha_out[...] = alpha_next
    alpha_inverse = 1.0 / as_column(alpha_next)
    for b in range(col_tiles):
        here = slice(b * tile, (b + 1) * tile)
        cell_out[:, here] = cell_out[:, here] * alpha_inverse


def per_device(rows, cols, sens_tiles, tile_coords, tile_counts, data_vec, cell_vec, alpha_now):
    slots, tile = sens_tiles.shape[0], sens_tiles.shape[1]
    samples, data_size = data_vec.shape
    cell_size = cell_vec.shape[1]
    row_tiles, col_tiles = data_size // tile, cell_size // tile
    halves = row_tiles // 2
    chunks = cell_size // CHUNK
    lanes = (samples + 127) // 128 * 128
    f32, bf16 = jnp.float32, jnp.bfloat16
    alpha_wide = jnp.pad(alpha_now, (0, lanes - samples)).reshape(1, lanes)
    half = pltpu.VMEM((halves, samples, tile), f32)
    part = pltpu.VMEM((chunks, samples, CHUNK), f32)
    dma = pltpu.SemaphoreType.DMA
    vmem = pl.BlockSpec(memory_space=pltpu.VMEM)
    smem = pl.BlockSpec(memory_space=pltpu.SMEM)
    hbm = pl.BlockSpec(memory_space=pl.ANY)
    data_next, cell_next, beta, alpha = pl.pallas_call(
        functools.partial(kernel, rows, cols),
        out_shape=(
            jax.ShapeDtypeStruct((samples, data_size), f32),
            jax.ShapeDtypeStruct((samples, cell_size), f32),
            jax.ShapeDtypeStruct((1, lanes), f32),
            jax.ShapeDtypeStruct((1, lanes), f32),
        ),
        in_specs=[smem, smem, vmem, hbm, hbm, hbm],
        out_specs=(vmem, vmem, vmem, vmem),
        scratch_shapes=[
            pltpu.SMEM((row_tiles * col_tiles,), jnp.int32),
            pltpu.SMEM((slots,), jnp.int32),
            pltpu.VMEM((slots + 1, tile, tile), bf16),
            pltpu.VMEM((samples, data_size), f32),
            pltpu.VMEM((samples, cell_size), f32),
            pltpu.VMEM((col_tiles, samples, tile), bf16),
            half, half, half, half, half, half, half,
            pltpu.VMEM((row_tiles, samples, tile), f32),
            pltpu.VMEM((row_tiles, samples, tile), bf16),
            part, part, part, part, part,
            pltpu.VMEM((samples, 128), f32),
            pltpu.VMEM((8, lanes), f32),
            pltpu.VMEM((rows, 8, lanes), f32),
            pltpu.VMEM((8, lanes), f32),
            pltpu.VMEM((cols, 8, lanes), f32),
            dma((3,)),
            dma((halves,)), dma((halves,)), dma((halves,)), dma((halves,)),
            dma((4, halves)),
            dma((4, chunks)),
            dma((2, rows)),
            dma((2, cols)),
        ],
        compiler_params=pltpu.CompilerParams(
            collective_id=0, has_side_effects=True, vmem_limit_bytes=40 * 2**20
        ),
    )(tile_coords, tile_counts, alpha_wide, sens_tiles, data_vec, cell_vec)
    return data_next, cell_next, beta[0, :samples], alpha[0, :samples]


def solution(mesh):
    placed = (
        P(("blocks", "rows"), "cols", None),
        P(("blocks", "rows"), "cols"),
        P(("blocks", "rows"), "cols"),
        P("blocks", "rows"),
        P("blocks", "cols"),
        P("blocks"),
    )
    return jax.shard_map(
        functools.partial(per_device, mesh.shape["rows"], mesh.shape["cols"]),
        mesh=mesh,
        in_specs=placed,
        out_specs=(P("blocks", "rows"), P("blocks", "cols"), P("blocks"), P("blocks")),
        check_vma=False,
    )
```

```python
import functools

import jax
import jax.numpy as jnp
from jax import lax
from jax.experimental import pallas as pl
from jax.experimental.pallas import tpu as pltpu
from jax.sharding import PartitionSpec as P

EPSILON = 1e-06
MESH = pl.DeviceIdType.MESH
HOP = 5
GROUPS = 1
PIECES = 3
WINDOW = 4
LOADS = 4


def remote(src, dst, send_sem, recv_sem, axis, peer):
    return pltpu.make_async_remote_copy(
        src_ref=src, dst_ref=dst, send_sem=send_sem, recv_sem=recv_sem, device_id={axis: peer}, device_id_type=MESH
    )


class Line:
    def __init__(self, count, place, axis, device_of, own, up, down, up_out, down_out, sems, window=0):
        self.count, self.place, self.axis, self.device_of = count, place, axis, device_of
        self.own, self.up, self.down, self.up_out, self.down_out = own, up, down, up_out, down_out
        self.up_send, self.up_recv, self.down_send, self.down_recv = sems
        self.chunks, self.window = own.shape[0], window

    def up_copy(self, src, i):
        peer = self.device_of(lax.rem(self.place + 1, self.count))
        return remote(src.at[i], self.up.at[i], self.up_send.at[i], self.up_recv.at[i], self.axis, peer)

    def down_copy(self, src, i):
        peer = self.device_of(lax.rem(self.place + self.count - 1, self.count))
        return remote(src.at[i], self.down.at[i], self.down_send.at[i], self.down_recv.at[i], self.axis, peer)

    def begin(self, i):
        @pl.when(self.place == 0)
        def _():
            self.up_copy(self.own, i).start()

        @pl.when(self.place == self.count - 1)
        def _():
            self.down_copy(self.own, i).start()

    def paced(self, copy, i):
        if self.window:

            @pl.when(i >= self.window)
            def _():
                copy(self.own, i - self.window).wait_send()

    def run(self, low, high, spread, finish):
        first, last = self.place == 0, self.place == self.count - 1
        from_below = self.place * spread
        from_above = (self.count - 1 - self.place) * spread

        def slot(s, carry):
            i = low + s - from_below

            @pl.when((i >= low) & (i < high))
            def _():
                if self.window:

                    @pl.when(first)
                    def _():
                        self.paced(self.up_copy, i)
                        self.up_copy(self.own, i).start()

                @pl.when(jnp.logical_not(first))
                def _():
                    self.up_copy(self.up_out, i).wait_recv()

                    @pl.when(jnp.logical_not(last))
                    def _():
                        self.up_out[i] = self.own[i] + self.up[i]
                        self.paced(self.up_copy, i)
                        self.up_copy(self.up_out, i).start()

            k = low + s - from_above

            @pl.when((k >= low) & (k < high))
            def _():
                if self.window:

                    @pl.when(last)
                    def _():
                        self.paced(self.down_copy, k)
                        self.down_copy(self.own, k).start()

                @pl.when(jnp.logical_not(last))
                def _():
                    self.down_copy(self.down_out, k).wait_recv()

                    @pl.when(jnp.logical_not(first))
                    def _():
                        self.down_out[k] = self.own[k] + self.down[k]
                        self.paced(self.down_copy, k)
                        self.down_copy(self.down_out, k).start()

            m = low + s - jnp.maximum(from_below, from_above)

            @pl.when((m >= low) & (m < high))
            def _():
                @pl.when(first)
                def _():
                    finish(m, self.own[m] + self.down[m])

                @pl.when(last)
                def _():
                    finish(m, self.up[m] + self.own[m])

                if self.count > 2:

                    @pl.when(jnp.logical_not(first | last))
                    def _():
                        finish(m, self.up_out[m] + self.down[m])

            return carry

        lax.fori_loop(0, high - low + (self.count - 1) * spread, slot, 0)

    def end(self):
        def one(i, carry):
            @pl.when(self.place < self.count - 1)
            def _():
                self.up_copy(self.own, i).wait_send()

            @pl.when(self.place > 0)
            def _():
                self.down_copy(self.own, i).wait_send()

            return carry

        lax.fori_loop(max(self.chunks - self.window, 0) if self.window else 0, self.chunks, one, 0)


def share_start(axis, count, me, row, out, got, send, recv):
    wide = jnp.broadcast_to(row, out.shape)
    out[...] = wide
    got[me] = wide

    def one(d, carry):
        peer = lax.rem(me + d, count)
        remote(out, got.at[me], send.at[d], recv.at[me], axis, peer).start()
        return carry

    lax.fori_loop(1, count, one, 0)


def share_end(axis, count, me, out, got, send, recv):
    def one(d, carry):
        peer = lax.rem(me + d, count)
        remote(out, got.at[peer], send.at[d], recv.at[peer], axis, peer).wait_recv()
        return carry

    lax.fori_loop(1, count, one, 0)

    def sent(d, carry):
        peer = lax.rem(me + d, count)
        remote(out, got.at[me], send.at[d], recv.at[me], axis, peer).wait_send()
        return carry

    lax.fori_loop(1, count, sent, 0)
    total = got[0]
    for j in range(1, count):
        total = total + got[j]
    return total[0:1]


def kernel(
    rows, cols, groups,
    coords, counts, alpha_in, tiles_in, data_in, cell_in,
    data_out, cell_out, beta_out, alpha_out,
    table, tiles, data, cell, cell_low, other, other_got, half, half_up, half_down, half_up_out, half_down_out,
    resid, part, part_up, part_down, part_up_out, part_down_out, squares, data_squares, beta_wide, inverse_wide,
    beta_row, beta_got, alpha_row, alpha_got,
    load_sems, pair_send, pair_recv, back_send, back_recv, half_sems, part_sems, beta_sems, alpha_sems,
):
    slots, tile = tiles_in.shape[0], tiles_in.shape[1]
    samples = data_in.shape[0]
    row_tiles, col_tiles = data_in.shape[1] // tile, cell_in.shape[1] // tile
    halves = row_tiles // 2
    size = samples // groups
    strip = size // PIECES
    r, c = lax.axis_index("rows"), lax.axis_index("cols")
    side = lax.rem(c, 2)
    group = c // 2
    partner = c + 1 - 2 * side

    barrier = pltpu.get_barrier_semaphore()

    def greet(axis, count, me):
        def one(d, carry):
            pl.semaphore_signal(barrier, inc=1, device_id={axis: lax.rem(me + d, count)}, device_id_type=MESH)
            return carry

        lax.fori_loop(1, count, one, 0)

    greet("rows", rows, r)
    greet("cols", cols, c)

    loads = [
        pltpu.make_async_copy(cell_in, cell, load_sems.at[0]),
        pltpu.make_async_copy(data_in, data, load_sems.at[1]),
    ]
    part_slots = slots // LOADS
    for e in range(LOADS):
        some = pl.ds(e * part_slots, part_slots)
        loads.append(pltpu.make_async_copy(tiles_in.at[some], tiles.at[some], load_sems.at[2 + e]))
    for load in loads:
        load.start()
    tiles[slots] = jnp.zeros(tiles.shape[1:], tiles.dtype)

    listed = counts[0, 0]
    keys = [jnp.where(t < listed, coords[0, t] * col_tiles + coords[1, t], -1) for t in range(slots)]

    def find(p, carry):
        found = jnp.int32(slots)
        for t in range(slots):
            found = jnp.where(keys[t] == p, t, found)
        table[p] = found
        return carry

    lax.fori_loop(0, row_tiles * col_tiles, find, 0)

    square = (samples, samples)
    eye = lax.broadcasted_iota(jnp.int32, square, 0) == lax.broadcasted_iota(jnp.int32, square, 1)

    def as_row(column):
        return jnp.sum(jnp.where(eye, column, 0.0), axis=0, keepdims=True)

    def as_column(row):
        return jnp.sum(jnp.where(eye, row, 0.0), axis=1, keepdims=True)

    def folded(block):
        piece = block[:, :128]
        for e in range(1, block.shape[1] // 128):
            piece = piece + block[:, e * 128:(e + 1) * 128]
        return piece

    alpha = as_column(alpha_in[...])
    squares[...] = jnp.zeros_like(squares)

    loads[0].wait()
    for b in range(col_tiles):
        cell_low[b] = cell[:, b * tile:(b + 1) * tile].astype(jnp.bfloat16)
    for load in loads[2:]:
        load.wait()

    across = Line(
        cols // 2, group, "cols", lambda q: q * 2 + side, half, half_up, half_down, half_up_out, half_down_out,
        [half_sems.at[i] for i in range(4)],
    )
    along = Line(
        rows, r, "rows", lambda q: q, part, part_up, part_down, part_up_out, part_down_out,
        [part_sems.at[i] for i in range(4)], WINDOW,
    )

    def span(g):
        return slice(g * size, (g + 1) * size)

    def forward(g, a):
        total = None
        for b in range(col_tiles):
            term = lax.dot_general(
                cell_low[b, span(g)], tiles[table[a * col_tiles + b]], (((1,), (1,)), ((), ())),
                preferred_element_type=jnp.float32,
            )
            total = term if total is None else total + term
        return total

    def pair_copy(i):
        return remote(other.at[i], other_got.at[i], pair_send.at[i], pair_recv.at[i], "cols", partner)

    def back_copy(g, a, i):
        here = resid.at[g * row_tiles + a]
        return remote(here, here, back_send.at[i], back_recv.at[i], "cols", partner)

    def multiply(g):
        for j in range(halves):
            i = g * halves + j
            other[i] = forward(g, (1 - side) * halves + j)
            if i == 0:
                pl.semaphore_wait(barrier, rows + cols - 2)
            pair_copy(i).start()
        for j in range(halves):
            half[g * halves + j] = forward(g, side * halves + j)

    def exchange(g):
        for j in range(halves):
            i = g * halves + j
            pair_copy(i).wait_recv()
            half[i] = half[i] + other_got[i]
            across.begin(i)

    def reduce(g):
        def finish(i, total):
            a = side * halves + i - g * halves
            here = pl.ds(pl.multiple_of(a * tile, tile), tile)
            resid[g * row_tiles + a] = total - alpha[span(g)] * data[span(g), here]
            back_copy(g, a, i).start()

        across.run(g * halves, (g + 1) * halves, 1, finish)

    def adjoin(g):
        for j in range(halves):
            back_copy(g, (1 - side) * halves + j, g * halves + j).wait_recv()
        low, sums = [], None
        for a in range(row_tiles):
            block = resid[g * row_tiles + a]
            low.append(block.astype(jnp.bfloat16))
            piece = folded(block * block)
            sums = piece if sums is None else sums + piece
        data_squares[span(g)] = sums
        for b in range(col_tiles):
            total = None
            for a in range(row_tiles):
                term = jnp.dot(low[a], tiles[table[a * col_tiles + b]], preferred_element_type=jnp.float32)
                total = term if total is None else total + term
            for e in range(PIECES):
                part[(g * col_tiles + b) * PIECES + e] = total[e * strip:(e + 1) * strip]

    multiply(0)
    if groups > 1:
        multiply(1)
    exchange(0)
    loads[1].wait()
    for g in range(groups):
        if g + 2 < groups:
            multiply(g + 2)
        if g + 1 < groups:
            exchange(g + 1)
        reduce(g)
        adjoin(g)

    sums = jnp.sum(data_squares[...], axis=1, keepdims=True)
    share_start("rows", rows, r, as_row(sums), beta_row, beta_got, beta_sems.at[0], beta_sems.at[1])

    data_total = jnp.float32(data_in.shape[1] * rows)
    cell_total = jnp.float32(cell_in.shape[1] * cols)

    def finish_cells(i, total):
        @pl.when(i == 0)
        def _():
            beta = jnp.sqrt(
                share_end("rows", rows, r, beta_row, beta_got, beta_sems.at[0], beta_sems.at[1]) / data_total + EPSILON
            )
            beta_out[...] = beta
            column = as_column(beta)
            beta_wide[...] = jnp.broadcast_to(column, beta_wide.shape)
            inverse_wide[...] = jnp.broadcast_to(1.0 / column, inverse_wide.shape)

        tiles_before, e = i // PIECES, lax.rem(i, PIECES)
        g, b = tiles_before // col_tiles, lax.rem(tiles_before, col_tiles)
        who = pl.ds(pl.multiple_of(g * size + e * strip, strip), strip)
        for q in range(tile // 128):
            here = pl.ds(pl.multiple_of(b * tile + q * 128, 128), 128)
            fresh = total[:, q * 128:(q + 1) * 128] * inverse_wide[who] - beta_wide[who] * cell[who, here]
            cell_out[who, here] = fresh
            squares[who] += fresh * fresh

    along.run(0, groups * col_tiles * PIECES, HOP, finish_cells)
    sums = jnp.sum(squares[...], axis=1, keepdims=True)
    share_start("cols", cols, c, as_row(sums), alpha_row, alpha_got, alpha_sems.at[0], alpha_sems.at[1])
    for g in range(groups):
        for a in range(row_tiles):
            inverse = inverse_wide[span(g), :1]
            data_out[span(g), a * tile:(a + 1) * tile] = resid[g * row_tiles + a] * inverse
    for g in range(groups):
        for j in range(halves):
            pair_copy(g * halves + j).wait_send()
            back_copy(g, side * halves + j, g * halves + j).wait_send()
    across.end()
    along.end()
    alpha_next = jnp.sqrt(
        share_end("cols", cols, c, alpha_row, alpha_got, alpha_sems.at[0], alpha_sems.at[1]) / cell_total + EPSILON
    )
    alpha_out[...] = alpha_next
    alpha_inverse = 1.0 / as_column(alpha_next)
    for b in range(col_tiles):
        here = slice(b * tile, (b + 1) * tile)
        cell_out[:, here] = cell_out[:, here] * alpha_inverse


def per_device(rows, cols, sens_tiles, tile_coords, tile_counts, data_vec, cell_vec, alpha_now):
    slots, tile = sens_tiles.shape[0], sens_tiles.shape[1]
    samples, data_size = data_vec.shape
    cell_size = cell_vec.shape[1]
    row_tiles, col_tiles = data_size // tile, cell_size // tile
    halves = row_tiles // 2
    groups = next(g for g in (GROUPS, 2, 1) if samples % (16 * g) == 0 or g == 1)
    size = samples // groups
    f32, bf16 = jnp.float32, jnp.bfloat16
    half = pltpu.VMEM((groups * halves, size, tile), f32)
    part = pltpu.VMEM((groups * col_tiles * PIECES, size // PIECES, tile), f32)
    column = pltpu.VMEM((samples, 128), f32)
    dma = pltpu.SemaphoreType.DMA
    pairs = dma((groups * halves,))
    vmem = pl.BlockSpec(memory_space=pltpu.VMEM)
    smem = pl.BlockSpec(memory_space=pltpu.SMEM)
    hbm = pl.BlockSpec(memory_space=pltpu.HBM)
    data_next, cell_next, beta, alpha = pl.pallas_call(
        functools.partial(kernel, rows, cols, groups),
        out_shape=(
            jax.ShapeDtypeStruct((samples, data_size), f32),
            jax.ShapeDtypeStruct((samples, cell_size), f32),
            jax.ShapeDtypeStruct((1, samples), f32),
            jax.ShapeDtypeStruct((1, samples), f32),
        ),
        in_specs=[smem, smem, vmem, hbm, hbm, hbm],
        out_specs=(vmem, vmem, vmem, vmem),
        scratch_shapes=[
            pltpu.SMEM((row_tiles * col_tiles,), jnp.int32),
            pltpu.VMEM((slots + 1, tile, tile), bf16),
            pltpu.VMEM((samples, data_size), f32),
            pltpu.VMEM((samples, cell_size), f32),
            pltpu.VMEM((col_tiles, samples, tile), bf16),
            half, half, half, half, half, half, half,
            pltpu.VMEM((groups * row_tiles, size, tile), f32),
            part, part, part, part, part,
            column, column, column, column,
            pltpu.VMEM((8, samples), f32),
            pltpu.VMEM((rows, 8, samples), f32),
            pltpu.VMEM((8, samples), f32),
            pltpu.VMEM((cols, 8, samples), f32),
            dma((2 + LOADS,)),
            pairs, pairs, pairs, pairs,
            dma((4, groups * halves)),
            dma((4, groups * col_tiles * PIECES)),
            dma((2, rows)),
            dma((2, cols)),
        ],
        compiler_params=pltpu.CompilerParams(
            collective_id=0, has_side_effects=True, vmem_limit_bytes=60 * 2**20
        ),
    )(tile_coords.T, tile_counts, alpha_now.reshape(1, samples), sens_tiles, data_vec, cell_vec)
    return data_next, cell_next, beta.reshape(samples), alpha.reshape(samples)


def solution(mesh):
    placed = (
        P(("blocks", "rows"), "cols", None),
        P(("blocks", "rows"), "cols"),
        P(("blocks", "rows"), "cols"),
        P("blocks", "rows"),
        P("blocks", "cols"),
        P("blocks"),
    )
    return jax.shard_map(
        functools.partial(per_device, mesh.shape["rows"], mesh.shape["cols"]),
        mesh=mesh,
        in_specs=placed,
        out_specs=(P("blocks", "rows"), P("blocks", "cols"), P("blocks"), P("blocks")),
        check_vma=False,
    )
```

```python
import functools

import jax
import jax.numpy as jnp
from jax import lax
from jax.experimental import pallas as pl
from jax.experimental.pallas import tpu as pltpu
from jax.sharding import PartitionSpec as P

EPSILON = 1e-06
MESH = pl.DeviceIdType.MESH
HOP = 5
GROUPS = 1
PIECES = 3
WINDOW = 4
LOADS = 4


def remote(src, dst, send_sem, recv_sem, axis, peer):
    return pltpu.make_async_remote_copy(
        src_ref=src, dst_ref=dst, send_sem=send_sem, recv_sem=recv_sem, device_id={axis: peer}, device_id_type=MESH
    )


class Line:
    def __init__(self, count, place, axis, device_of, own, up, down, up_out, down_out, sems, window=0):
        self.count, self.place, self.axis, self.device_of = count, place, axis, device_of
        self.own, self.up, self.down, self.up_out, self.down_out = own, up, down, up_out, down_out
        self.up_send, self.up_recv, self.down_send, self.down_recv = sems
        self.chunks, self.window = own.shape[0], window

    def up_copy(self, src, i):
        peer = self.device_of(lax.rem(self.place + 1, self.count))
        return remote(src.at[i], self.up.at[i], self.up_send.at[i], self.up_recv.at[i], self.axis, peer)

    def down_copy(self, src, i):
        peer = self.device_of(lax.rem(self.place + self.count - 1, self.count))
        return remote(src.at[i], self.down.at[i], self.down_send.at[i], self.down_recv.at[i], self.axis, peer)

    def begin(self, i):
        @pl.when(self.place == 0)
        def _():
            self.up_copy(self.own, i).start()

        @pl.when(self.place == self.count - 1)
        def _():
            self.down_copy(self.own, i).start()

    def paced(self, copy, i):
        if self.window:

            @pl.when(i >= self.window)
            def _():
                copy(self.own, i - self.window).wait_send()

    def run(self, low, high, spread, finish):
        first, last = self.place == 0, self.place == self.count - 1
        from_below = self.place * spread
        from_above = (self.count - 1 - self.place) * spread

        def slot(s, carry):
            i = low + s - from_below

            @pl.when((i >= low) & (i < high))
            def _():
                if self.window:

                    @pl.when(first & (i >= self.window))
                    def _():
                        self.paced(self.up_copy, i)
                        self.up_copy(self.own, i).start()

                @pl.when(jnp.logical_not(first))
                def _():
                    self.up_copy(self.up_out, i).wait_recv()

                    @pl.when(jnp.logical_not(last))
                    def _():
                        self.up_out[i] = self.own[i] + self.up[i]
                        self.paced(self.up_copy, i)
                        self.up_copy(self.up_out, i).start()

            k = low + s - from_above

            @pl.when((k >= low) & (k < high))
            def _():
                if self.window:

                    @pl.when(last & (k >= self.window))
                    def _():
                        self.paced(self.down_copy, k)
                        self.down_copy(self.own, k).start()

                @pl.when(jnp.logical_not(last))
                def _():
                    self.down_copy(self.down_out, k).wait_recv()

                    @pl.when(jnp.logical_not(first))
                    def _():
                        self.down_out[k] = self.own[k] + self.down[k]
                        self.paced(self.down_copy, k)
                        self.down_copy(self.down_out, k).start()

            m = low + s - jnp.maximum(from_below, from_above)

            @pl.when((m >= low) & (m < high))
            def _():
                @pl.when(first)
                def _():
                    finish(m, self.own[m] + self.down[m])

                @pl.when(last)
                def _():
                    finish(m, self.up[m] + self.own[m])

                if self.count > 2:

                    @pl.when(jnp.logical_not(first | last))
                    def _():
                        finish(m, self.up_out[m] + self.down[m])

            return carry

        lax.fori_loop(0, high - low + (self.count - 1) * spread, slot, 0)

    def end(self):
        def one(i, carry):
            @pl.when(self.place < self.count - 1)
            def _():
                self.up_copy(self.own, i).wait_send()

            @pl.when(self.place > 0)
            def _():
                self.down_copy(self.own, i).wait_send()

            return carry

        lax.fori_loop(max(self.chunks - self.window, 0) if self.window else 0, self.chunks, one, 0)


def share_start(axis, count, me, row, out, got, send, recv):
    wide = jnp.broadcast_to(row, out.shape)
    out[...] = wide
    got[me] = wide

    def one(d, carry):
        peer = lax.rem(me + d, count)
        remote(out, got.at[me], send.at[d], recv.at[me], axis, peer).start()
        return carry

    lax.fori_loop(1, count, one, 0)


def share_end(axis, count, me, out, got, send, recv):
    def one(d, carry):
        peer = lax.rem(me + d, count)
        remote(out, got.at[peer], send.at[d], recv.at[peer], axis, peer).wait_recv()
        return carry

    lax.fori_loop(1, count, one, 0)

    def sent(d, carry):
        peer = lax.rem(me + d, count)
        remote(out, got.at[me], send.at[d], recv.at[me], axis, peer).wait_send()
        return carry

    lax.fori_loop(1, count, sent, 0)
    total = got[0]
    for j in range(1, count):
        total = total + got[j]
    return total[0:1]


def kernel(
    rows, cols, groups,
    coords, counts, alpha_in, tiles_in, data_in, cell_in,
    data_out, cell_out, norms_out,
    table, tiles, data, cell, cell_low, other, other_got, half, half_up, half_down, half_up_out, half_down_out,
    resid, part, part_up, part_down, part_up_out, part_down_out, squares, data_squares, beta_wide, inverse_wide,
    beta_row, beta_got, alpha_row, alpha_got,
    load_sems, pair_send, pair_recv, back_send, back_recv, half_sems, part_sems, beta_sems, alpha_sems,
):
    slots, tile = tiles_in.shape[0], tiles_in.shape[1]
    samples = data_in.shape[0]
    row_tiles, col_tiles = data_in.shape[1] // tile, cell_in.shape[1] // tile
    halves = row_tiles // 2
    size = samples // groups
    strip = size // PIECES
    r, c = lax.axis_index("rows"), lax.axis_index("cols")
    side = lax.rem(c, 2)
    group = c // 2
    partner = c + 1 - 2 * side

    barrier = pltpu.get_barrier_semaphore()

    def greet(axis, count, me):
        def one(d, carry):
            pl.semaphore_signal(barrier, inc=1, device_id={axis: lax.rem(me + d, count)}, device_id_type=MESH)
            return carry

        lax.fori_loop(1, count, one, 0)

    greet("rows", rows, r)
    greet("cols", cols, c)

    loads = [
        pltpu.make_async_copy(cell_in, cell, load_sems.at[0]),
        pltpu.make_async_copy(data_in, data, load_sems.at[1]),
    ]
    part_slots = slots // LOADS
    for e in range(LOADS):
        some = pl.ds(e * part_slots, part_slots)
        loads.append(pltpu.make_async_copy(tiles_in.at[some], tiles.at[some], load_sems.at[2 + e]))
    for load in loads:
        load.start()
    tiles[slots] = jnp.zeros(tiles.shape[1:], tiles.dtype)

    listed = counts[0, 0]
    keys = [jnp.where(t < listed, coords[0, t] * col_tiles + coords[1, t], -1) for t in range(slots)]

    def find(p, carry):
        found = jnp.int32(slots)
        for t in range(slots):
            found = jnp.where(keys[t] == p, t, found)
        table[p] = found
        return carry

    lax.fori_loop(0, row_tiles * col_tiles, find, 0)

    square = (samples, samples)
    eye = lax.broadcasted_iota(jnp.int32, square, 0) == lax.broadcasted_iota(jnp.int32, square, 1)

    def as_row(column):
        return jnp.sum(jnp.where(eye, column, 0.0), axis=0, keepdims=True)

    def as_column(row):
        return jnp.sum(jnp.where(eye, row, 0.0), axis=1, keepdims=True)

    def folded(block):
        piece = block[:, :128]
        for e in range(1, block.shape[1] // 128):
            piece = piece + block[:, e * 128:(e + 1) * 128]
        return piece

    alpha = as_column(alpha_in[...])
    squares[...] = jnp.zeros_like(squares)

    loads[0].wait()
    for b in range(col_tiles):
        cell_low[b] = cell[:, b * tile:(b + 1) * tile].astype(jnp.bfloat16)
    for load in loads[2:]:
        load.wait()

    across = Line(
        cols // 2, group, "cols", lambda q: q * 2 + side, half, half_up, half_down, half_up_out, half_down_out,
        [half_sems.at[i] for i in range(4)],
    )
    along = Line(
        rows, r, "rows", lambda q: q, part, part_up, part_down, part_up_out, part_down_out,
        [part_sems.at[i] for i in range(4)], WINDOW,
    )

    def span(g):
        return slice(g * size, (g + 1) * size)

    def forward(g, a):
        total = None
        for b in range(col_tiles):
            term = lax.dot_general(
                cell_low[b, span(g)], tiles[table[a * col_tiles + b]], (((1,), (1,)), ((), ())),
                preferred_element_type=jnp.float32,
            )
            total = term if total is None else total + term
        return total

    def pair_copy(i):
        return remote(other.at[i], other_got.at[i], pair_send.at[i], pair_recv.at[i], "cols", partner)

    def back_copy(g, a, i):
        here = resid.at[g * row_tiles + a]
        return remote(here, here, back_send.at[i], back_recv.at[i], "cols", partner)

    def multiply(g):
        for j in range(halves):
            i = g * halves + j
            other[i] = forward(g, (1 - side) * halves + j)
            if i == 0:
                pl.semaphore_wait(barrier, rows + cols - 2)
            pair_copy(i).start()
        for j in range(halves):
            half[g * halves + j] = forward(g, side * halves + j)

    def exchange(g):
        for j in range(halves):
            i = g * halves + j
            pair_copy(i).wait_recv()
            half[i] = half[i] + other_got[i]
            across.begin(i)

    def reduce(g):
        def finish(i, total):
            a = side * halves + i - g * halves
            here = pl.ds(pl.multiple_of(a * tile, tile), tile)
            resid[g * row_tiles + a] = total - alpha[span(g)] * data[span(g), here]
            back_copy(g, a, i).start()

        across.run(g * halves, (g + 1) * halves, 1, finish)

    def adjoin(g):
        for j in range(halves):
            back_copy(g, (1 - side) * halves + j, g * halves + j).wait_recv()
        low, sums = [], None
        for a in range(row_tiles):
            block = resid[g * row_tiles + a]
            low.append(block.astype(jnp.bfloat16))
            piece = folded(block * block)
            sums = piece if sums is None else sums + piece
        data_squares[span(g)] = sums
        for b in range(col_tiles):
            total = None
            for a in range(row_tiles):
                term = jnp.dot(low[a], tiles[table[a * col_tiles + b]], preferred_element_type=jnp.float32)
                total = term if total is None else total + term
            for e in range(PIECES):
                i = (g * col_tiles + b) * PIECES + e
                part[i] = total[e * strip:(e + 1) * strip]
                if i < WINDOW:
                    along.begin(i)

    multiply(0)
    if groups > 1:
        multiply(1)
    exchange(0)
    loads[1].wait()
    for g in range(groups):
        if g + 2 < groups:
            multiply(g + 2)
        if g + 1 < groups:
            exchange(g + 1)
        reduce(g)
        adjoin(g)

    sums = jnp.sum(data_squares[...], axis=1, keepdims=True)
    share_start("rows", rows, r, as_row(sums), beta_row, beta_got, beta_sems.at[0], beta_sems.at[1])

    data_total = jnp.float32(data_in.shape[1] * rows)
    cell_total = jnp.float32(cell_in.shape[1] * cols)

    def finish_cells(i, total):
        @pl.when(i == 0)
        def _():
            beta = jnp.sqrt(
                share_end("rows", rows, r, beta_row, beta_got, beta_sems.at[0], beta_sems.at[1]) / data_total + EPSILON
            )
            norms_out[0:1] = beta
            column = as_column(beta)
            beta_wide[...] = jnp.broadcast_to(column, beta_wide.shape)
            inverse_wide[...] = jnp.broadcast_to(1.0 / column, inverse_wide.shape)

        tiles_before, e = i // PIECES, lax.rem(i, PIECES)
        g, b = tiles_before // col_tiles, lax.rem(tiles_before, col_tiles)
        who = pl.ds(pl.multiple_of(g * size + e * strip, strip), strip)
        for q in range(tile // 128):
            here = pl.ds(pl.multiple_of(b * tile + q * 128, 128), 128)
            fresh = total[:, q * 128:(q + 1) * 128] * inverse_wide[who] - beta_wide[who] * cell[who, here]
            cell_out[who, here] = fresh
            squares[who] += fresh * fresh

    along.run(0, groups * col_tiles * PIECES, HOP, finish_cells)
    sums = jnp.sum(squares[...], axis=1, keepdims=True)
    share_start("cols", cols, c, as_row(sums), alpha_row, alpha_got, alpha_sems.at[0], alpha_sems.at[1])
    for g in range(groups):
        for a in range(row_tiles):
            data_out[span(g), a * tile:(a + 1) * tile] = resid[g * row_tiles + a]
    for g in range(groups):
        for j in range(halves):
            pair_copy(g * halves + j).wait_send()
            back_copy(g, side * halves + j, g * halves + j).wait_send()
    across.end()
    along.end()
    alpha_next = jnp.sqrt(
        share_end("cols", cols, c, alpha_row, alpha_got, alpha_sems.at[0], alpha_sems.at[1]) / cell_total + EPSILON
    )
    norms_out[1:2] = alpha_next


def per_device(rows, cols, sens_tiles, tile_coords, tile_counts, data_vec, cell_vec, alpha_now):
    slots, tile = sens_tiles.shape[0], sens_tiles.shape[1]
    samples, data_size = data_vec.shape
    cell_size = cell_vec.shape[1]
    row_tiles, col_tiles = data_size // tile, cell_size // tile
    halves = row_tiles // 2
    groups = next(g for g in (GROUPS, 2, 1) if samples % (16 * g) == 0 or g == 1)
    size = samples // groups
    f32, bf16 = jnp.float32, jnp.bfloat16
    half = pltpu.VMEM((groups * halves, size, tile), f32)
    part = pltpu.VMEM((groups * col_tiles * PIECES, size // PIECES, tile), f32)
    column = pltpu.VMEM((samples, 128), f32)
    dma = pltpu.SemaphoreType.DMA
    pairs = dma((groups * halves,))
    vmem = pl.BlockSpec(memory_space=pltpu.VMEM)
    smem = pl.BlockSpec(memory_space=pltpu.SMEM)
    hbm = pl.BlockSpec(memory_space=pltpu.HBM)
    data_next, cell_next, norms = pl.pallas_call(
        functools.partial(kernel, rows, cols, groups),
        out_shape=(
            jax.ShapeDtypeStruct((samples, data_size), f32),
            jax.ShapeDtypeStruct((samples, cell_size), f32),
            jax.ShapeDtypeStruct((2, samples), f32),
        ),
        in_specs=[smem, smem, vmem, hbm, hbm, hbm],
        out_specs=(vmem, vmem, vmem),
        scratch_shapes=[
            pltpu.SMEM((row_tiles * col_tiles,), jnp.int32),
            pltpu.VMEM((slots + 1, tile, tile), bf16),
            pltpu.VMEM((samples, data_size), f32),
            pltpu.VMEM((samples, cell_size), f32),
            pltpu.VMEM((col_tiles, samples, tile), bf16),
            half, half, half, half, half, half, half,
            pltpu.VMEM((groups * row_tiles, size, tile), f32),
            part, part, part, part, part,
            column, column, column, column,
            pltpu.VMEM((8, samples), f32),
            pltpu.VMEM((rows, 8, samples), f32),
            pltpu.VMEM((8, samples), f32),
            pltpu.VMEM((cols, 8, samples), f32),
            dma((2 + LOADS,)),
            pairs, pairs, pairs, pairs,
            dma((4, groups * halves)),
            dma((4, groups * col_tiles * PIECES)),
            dma((2, rows)),
            dma((2, cols)),
        ],
        compiler_params=pltpu.CompilerParams(
            collective_id=0, has_side_effects=True, vmem_limit_bytes=52 * 2**20
        ),
    )(tile_coords.T, tile_counts, alpha_now.reshape(1, samples), sens_tiles, data_vec, cell_vec)
    beta, alpha = norms[0], norms[1]
    return data_next / beta[:, None], cell_next / alpha[:, None], beta, alpha


def solution(mesh):
    placed = (
        P(("blocks", "rows"), "cols", None),
        P(("blocks", "rows"), "cols"),
        P(("blocks", "rows"), "cols"),
        P("blocks", "rows"),
        P("blocks", "cols"),
        P("blocks"),
    )
    return jax.shard_map(
        functools.partial(per_device, mesh.shape["rows"], mesh.shape["cols"]),
        mesh=mesh,
        in_specs=placed,
        out_specs=(P("blocks", "rows"), P("blocks", "cols"), P("blocks"), P("blocks")),
        check_vma=False,
    )
```
